512 devices in a mesh: grp: 16 (over z, core), ctx: 32 (over y, x).
Axes of the slice: x: 4, y: 8, z: 8, core: 2. Of those that a mesh axis runs over, the one named last changes fastest.
Arguments:
- q_resp: bfloat16 [32768, 4096], P(('grp', 'ctx')), parts along dimension 0, may hold values from -6 to 6
- k_resp: bfloat16 [32768, 512], P(('grp', 'ctx')), parts along dimension 0, may hold values from -6 to 6
- v_resp: bfloat16 [32768, 512], P(('grp', 'ctx')), parts along dimension 0, may hold values from -6 to 6
- k_prompt: bfloat16 [32768, 512], P(('grp', 'ctx')), parts along dimension 0, may hold values from -6 to 6
- v_prompt: bfloat16 [32768, 512], P(('grp', 'ctx')), parts along dimension 0, may hold values from -6 to 6
- d_out: bfloat16 [32768, 4096], P(('grp', 'ctx')), parts along dimension 0, may hold values from -6 to 6
- owner: int32 [512], P('grp'), parts along dimension 0, may hold values from 0 to 31, each once
- lengths: int32 [512], P('grp'), parts along dimension 0, may hold values from 16 to 64, as said below
- visible: int32 [512], P('grp'), parts along dimension 0, may hold values from 1024 to 2048, as said below
Outputs:
- out: bfloat16 [32768, 4096], P(('grp', 'ctx')), parts along dimension 0
- dq: bfloat16 [32768, 4096], P(('grp', 'ctx')), parts along dimension 0
- dk_prompt: bfloat16 [32768, 512], P(('grp', 'ctx')), parts along dimension 0
- dv_prompt: bfloat16 [32768, 512], P(('grp', 'ctx')), parts along dimension 0
- dk_resp: bfloat16 [32768, 512], P(('grp', 'ctx')), parts along dimension 0
- dv_resp: bfloat16 [32768, 512], P(('grp', 'ctx')), parts along dimension 0
The draws below stay inside these ranges and needn't reach their ends.
There are 16 independent parts, one for each index of `grp`. The reference program is written for one: setup_inputs(seed, part) draws one part's arguments, and reference() takes and returns one part's arrays. A program takes and returns all parts, laid end to end along the dimension named above; each array names one. Nothing has to cross between parts.
Inputs may be any that keep to these rules, and one draw needn't show every extreme that they name: `lengths`: some response fills all 64 positions of its window. `visible`: some response attends to the whole prompt.
All inputs are finite; a program needn't handle non-finite values.
Results may differ from the reference program's by a relative error of at most 0.022.
Values may be sent and summed in bfloat16 or wider, within the bound.
A program may use at most 128 MiB of HBM per device.

```python
import math
import jax
import jax.numpy as jnp
from jax import lax

H = 32
G = 4
HD = 128
RK = 64
NRESP = 32
PROMPT = 2048


def draw_q_resp(key, part):
    key = jax.random.fold_in(key, 11)
    values = jnp.clip(jax.random.normal(key, (NRESP * RK, H * HD), jnp.float32), -6.0, 6.0)
    return values.astype(jnp.bfloat16)


def draw_k_prompt(key, part):
    key = jax.random.fold_in(key, 12)
    values = jnp.clip(jax.random.normal(key, (PROMPT, G * HD), jnp.float32), -6.0, 6.0)
    return values.astype(jnp.bfloat16)


def draw_lengths(key, part):
    key = jax.random.fold_in(key, 21)
    first_key, second_key = jax.random.split(key)
    drawn = jax.random.randint(first_key, (NRESP,), RK // 4, RK + 1)
    chosen = jax.random.randint(second_key, (), 0, NRESP)
    return jnp.where(jnp.arange(NRESP) == chosen, RK, drawn).astype(jnp.int32)


def draw_visible(key, part):
    key = jax.random.fold_in(key, 31)
    first_key, second_key = jax.random.split(key)
    drawn = jax.random.randint(first_key, (NRESP,), PROMPT // 2, PROMPT + 1)
    chosen = jax.random.randint(second_key, (), 0, NRESP)
    return jnp.where(jnp.arange(NRESP) == chosen, PROMPT, drawn).astype(jnp.int32)


def block_scale(rng, extent, cuts, smallest, high):
    factor_of, own = 1.0, jax.random.fold_in(rng, 6)
    for position, blocks in cuts:
        draws = jnp.exp(jax.random.uniform(jax.random.fold_in(own, position), (blocks,), jnp.float32, smallest / len(cuts), high / len(cuts)))
        factor_of = factor_of * jnp.repeat(draws, extent[position] // blocks).reshape([-1 if axis == position else 1 for axis in range(len(extent))])
    return factor_of


def scatter_about(rng, shape, spread, reach, cuts=(), kind=jnp.bfloat16):
    gain = block_scale(rng, shape, cuts, -0.22, 0.18) if cuts else 1.0
    entries = jax.random.normal(rng, shape, jnp.float32) * spread * gain
    return jnp.minimum(jnp.maximum(entries, -reach), reach).astype(kind)


def setup_inputs(seed: int = 0, part: int = 0) -> dict:
    streams_of = jax.random.split(jax.random.key(seed), 10)
    part_keys = jax.random.split(jax.random.fold_in(streams_of[9], part), 10)
    return {
        "q_resp": draw_q_resp(jax.random.fold_in(jax.random.fold_in(streams_of[9], part), 71), part),
        "k_resp": scatter_about(part_keys[1], (NRESP * RK, G * HD), 1.0, 6.0, ((0, 32),)),
        "v_resp": scatter_about(part_keys[2], (NRESP * RK, G * HD), 1.0, 6.0, ((0, 32),)),
        "k_prompt": draw_k_prompt(jax.random.fold_in(jax.random.fold_in(streams_of[9], part), 71), part),
        "v_prompt": scatter_about(part_keys[4], (PROMPT, G * HD), 1.0, 6.0, ((0, 32),)),
        "d_out": scatter_about(part_keys[5], (NRESP * RK, H * HD), 1.0, 6.0, ((0, 32),)),
        "owner": jax.random.permutation(part_keys[6], NRESP).astype(jnp.int32),
        "lengths": draw_lengths(jax.random.fold_in(jax.random.fold_in(streams_of[9], part), 71), part),
        "visible": draw_visible(jax.random.fold_in(jax.random.fold_in(streams_of[9], part), 71), part),
    }


NEG_FILL = -1e+30

def slot_tables(owner, lengths, visible, shards):
    matching = owner[None, :] == jnp.arange(shards, dtype=jnp.int32)[:, None]
    slot_length = lax.optimization_barrier(jnp.sum(jnp.where(matching, lengths[None, :], 0), axis=1)).astype(jnp.int32)
    slot_visible = lax.optimization_barrier(jnp.sum(jnp.where(matching, visible[None, :], 0), axis=1)).astype(jnp.int32)
    return (slot_length, slot_visible)

def bfloat_round(values):
    return lax.optimization_barrier(values.astype(jnp.bfloat16)).astype(jnp.float32)

def softmax_block(scores, allowed):
    block_max = lax.optimization_barrier(jnp.max(jnp.where(allowed, scores, NEG_FILL), axis=-1))
    weights = jnp.where(allowed, jnp.exp(scores - block_max[..., None]), 0.0)
    return (block_max, weights, lax.optimization_barrier(jnp.sum(weights, axis=-1)))

def grads_block(scores, allowed, log_norm, row_delta, queries, grads, keys, values, score_scale):
    probability = jnp.where(allowed, jnp.exp(scores - log_norm[..., None]), 0.0)
    value_grad = jnp.einsum('qgrk,qgrd->kgd', bfloat_round(probability), grads)
    prob_grad = jnp.einsum('qgrd,kgd->qgrk', grads, values)
    score_grad = bfloat_round(probability * (prob_grad - row_delta[..., None]))
    query_grad = jnp.einsum('qgrk,kgd->qgrd', score_grad, keys) * score_scale
    key_grad = jnp.einsum('qgrk,qgrd->kgd', score_grad, queries) * score_scale
    return (query_grad, key_grad, value_grad)

def reference(q_resp, k_resp, v_resp, k_prompt, v_prompt, d_out, owner, lengths, visible):
    heads_per = H // G
    score_scale = 1.0 / math.sqrt(HD)
    slot_length, slot_visible = slot_tables(owner, lengths, visible, NRESP)
    prompt_keys = k_prompt.astype(jnp.float32).reshape(PROMPT, G, HD)
    prompt_values = v_prompt.astype(jnp.float32).reshape(PROMPT, G, HD)
    queries = q_resp.astype(jnp.float32).reshape(NRESP, RK, G, heads_per, HD)
    grads_out = d_out.astype(jnp.float32).reshape(NRESP, RK, G, heads_per, HD)
    window_keys = k_resp.astype(jnp.float32).reshape(NRESP, RK, G, HD)
    window_values = v_resp.astype(jnp.float32).reshape(NRESP, RK, G, HD)
    prompt_pos = jnp.arange(PROMPT, dtype=jnp.int32)
    key_pos = jnp.arange(RK, dtype=jnp.int32)

    def one_response(carry, inputs):
        key_total, value_total = carry
        rows_q, rows_g, keys_w, values_w, length, seen = inputs
        prompt_allowed = (prompt_pos < seen)[None, None, None, :]
        window_allowed = ((key_pos[None, :] >= RK - length) & (key_pos[None, :] <= key_pos[:, None]))[:, None, None, :]
        prompt_scores = jnp.einsum('qgrd,kgd->qgrk', rows_q, prompt_keys) * score_scale
        window_scores = jnp.einsum('qgrd,kgd->qgrk', rows_q, keys_w) * score_scale
        prompt_max, prompt_weights, prompt_sum = softmax_block(prompt_scores, prompt_allowed)
        prompt_out = jnp.einsum('qgrk,kgd->qgrd', bfloat_round(prompt_weights), prompt_values)
        window_max, window_weights, window_sum = softmax_block(window_scores, window_allowed)
        window_out = jnp.einsum('qgrk,kgd->qgrd', bfloat_round(window_weights), values_w)
        overall = jnp.maximum(prompt_max, window_max)
        prompt_factor = jnp.exp(prompt_max - overall)
        window_factor = jnp.exp(window_max - overall)
        denominator = prompt_factor * prompt_sum + window_factor * window_sum
        attended = (prompt_factor[..., None] * prompt_out + window_factor[..., None] * window_out) / denominator[..., None]
        log_norm = overall + jnp.log(denominator)
        row_delta = lax.optimization_barrier(jnp.sum(rows_g * attended, axis=-1))
        out_rows = attended.reshape(RK, H * HD).astype(jnp.bfloat16)
        prompt_q, prompt_k, prompt_v = grads_block(prompt_scores, prompt_allowed, log_norm, row_delta, rows_q, rows_g, prompt_keys, prompt_values, score_scale)
        window_q, window_k, window_v = grads_block(window_scores, window_allowed, log_norm, row_delta, rows_q, rows_g, keys_w, values_w, score_scale)
        dq_rows = (prompt_q + window_q).reshape(RK, H * HD).astype(jnp.bfloat16)
        results = (out_rows, dq_rows, window_k.reshape(RK, G * HD).astype(jnp.bfloat16), window_v.reshape(RK, G * HD).astype(jnp.bfloat16))
        return ((key_total + bfloat_round(prompt_k), value_total + bfloat_round(prompt_v)), results)
    start = jnp.zeros((PROMPT, G, HD), jnp.float32)
    (key_total, value_total), (outs, dqs, dks, dvs) = lax.scan(one_response, (start, start), (queries, grads_out, window_keys, window_values, slot_length, slot_visible))
    out = outs.reshape(NRESP * RK, H * HD)
    dq = dqs.reshape(NRESP * RK, H * HD)
    dk_prompt = key_total.reshape(PROMPT, G * HD).astype(jnp.bfloat16)
    dv_prompt = value_total.reshape(PROMPT, G * HD).astype(jnp.bfloat16)
    dk_resp = dks.reshape(NRESP * RK, G * HD)
    dv_resp = dvs.reshape(NRESP * RK, G * HD)
    return (out, dq, dk_prompt, dv_prompt, dk_resp, dv_resp)
```

```python
import functools
import math

import jax
import jax.numpy as jnp
from jax import lax
from jax.experimental import pallas as pl
from jax.experimental.pallas import tpu as pltpu
from jax.sharding import PartitionSpec as P

H = 32
G = 4
HD = 128
HPG = H // G
GW = HPG * HD
X = 4
Y = 8
W = 64
ROWS = HPG * W
CHUNK = X * W
NEG = -1e30
SCALE = 1.0 / math.sqrt(HD)
LOG2 = SCALE * math.log2(math.e)
MESH = pl.DeviceIdType.MESH
BF = jnp.bfloat16
F32 = jnp.float32
UP, DOWN = 0, 1
PIECES = 2
PIECE = CHUNK // PIECES
OFF = (0, 1, 3, 2)
SLOT = (0, 1, 3, 2)


def dot(a, b):
    return lax.dot_general(a, b, (((1,), (0,)), ((), ())), preferred_element_type=F32)


def kernel(
    owner, lengths, visible, q, kr, vr, kp, vp, do,
    out, dq, dkp, dvp, dkr, dvr,
    slots, qb, dob, krb, vrb, kv, kt, vt, qt, dot_t, eb, wb, mb, mcur, oacc, stat,
    dqacc, dkacc, dvacc, outs, dqs, dkrs, dvrs, rs_s, rs_r, fin,
    in_ls, in_ss, in_rs, ag_ss, ag_rs, out_ls, out_ss, out_rs, rs_ss, rs_rs,
):
    c = lax.axis_index("ctx")
    y = c // X
    x = lax.rem(c, X)

    def peer(d):
        return {"ctx": y * X + lax.rem(x + d, X)}

    def ring(direction):
        return {"ctx": lax.rem(y + (1 if direction == UP else Y - 1), Y) * X + x}

    barrier = pltpu.get_barrier_semaphore()
    for device in (peer(1), peer(2), peer(3), ring(UP), ring(DOWN)):
        pl.semaphore_signal(barrier, inc=1, device_id=device, device_id_type=MESH)

    sources = ((kp, HD), (vp, HD), (kr, HD), (vr, HD), (q, GW), (do, GW))

    def landing(kind, slot):
        if kind < 2:
            return kv.at[0, slot, kind]
        return (krb, vrb, qb, dob)[kind - 2].at[slot]

    def enter(kind, d):
        ref, width = sources[kind]
        column = pl.multiple_of(lax.rem(x + d, X) * width, HD)
        return pltpu.make_async_remote_copy(
            src_ref=ref.at[:, pl.ds(column, width)],
            dst_ref=landing(kind, SLOT[X - d]),
            send_sem=in_ss.at[kind, d - 1],
            recv_sem=in_rs.at[kind, d - 1],
            device_id=peer(d),
            device_id_type=MESH,
        )

    def enter_own(kind):
        ref, width = sources[kind]
        column = pl.multiple_of(x * width, HD)
        return pltpu.make_async_copy(
            ref.at[:, pl.ds(column, width)], landing(kind, 0), in_ls.at[kind]
        )

    def entered(kind, i):
        if i == 0:
            enter_own(kind).wait()
        else:
            enter(kind, X - OFF[i]).wait_recv()

    for kind in range(6):
        enter_own(kind).start()

    for i in range(X):
        holder = y * X + lax.rem(x + OFF[i], X)

        def count(j, carry, holder=holder):
            hit = owner[j] == holder
            return (
                carry[0] + jnp.where(hit, lengths[j], 0),
                carry[1] + jnp.where(hit, visible[j], 0),
            )

        length, seen = lax.fori_loop(0, Y * X, count, (jnp.int32(0), jnp.int32(0)))
        slots[0, i] = length
        slots[1, i] = seen

    pl.semaphore_wait(barrier, 5)
    for kind in range(6):
        for d in (1, 3, 2):
            enter(kind, d).start()

    def gather(hop, direction, i):
        away = (1 - hop) % Y if direction == UP else hop - 1
        there = -hop % Y if direction == UP else hop
        src, dst = kv.at[away, i], kv.at[there, i]
        if hop == 4:
            src, dst = kv.at[away, i, direction], kv.at[there, i, direction]
        return pltpu.make_async_remote_copy(
            src_ref=src,
            dst_ref=dst,
            send_sem=ag_ss.at[hop - 1, direction, i],
            recv_sem=ag_rs.at[hop - 1, direction, i],
            device_id=ring(direction),
            device_id_type=MESH,
        )

    def spread(i):
        for kind in (0, 1):
            entered(kind, i)
        for direction in (UP, DOWN):
            gather(1, direction, i).start()

    def hop_on(hop, i):
        for direction in (UP, DOWN):
            gather(hop, direction, i).wait_recv()
            if hop < 4:
                gather(hop + 1, direction, i).start()

    def turn(a):
        kt[a] = kv[a, :, 0].reshape(CHUNK, HD).T
        vt[a, 0:HD, :] = kv[a, :, 1].reshape(CHUNK, HD).T
        vt[a, HD:, :] = jnp.ones((16, CHUNK), BF)

    def natural(ref, i):
        return jnp.concatenate([ref[i, :, n * HD : (n + 1) * HD] for n in range(HPG)], axis=0)

    def chunks_of(step):
        return (step,) if step in (0, 4) else (Y - step, step)

    def soften(i, step, scores, values_t, keep):
        top = functools.reduce(
            jnp.maximum, [jnp.max(s, axis=0, keepdims=True) for s in scores]
        )
        if step is not None:
            before = mcur[i]
            top = jnp.maximum(top, before)
        mcur[i] = top
        mb[i, 5 if step is None else step] = top
        total = None
        for s, values, ref in zip(scores, values_t, keep):
            e = jnp.exp2((s - top) * LOG2).astype(BF)
            ref[...] = e
            term = dot(values, e)
            total = term if total is None else total + term
        if step is None:
            oacc[i] = total
        else:
            oacc[i] = oacc[i] * jnp.exp2((before - top) * LOG2) + total

    def ready(i):
        for kind in (2, 3, 4):
            entered(kind, i)
        qt[i] = natural(qb, i).T
        key = lax.broadcasted_iota(jnp.int32, (W, ROWS), 0)
        query = lax.rem(lax.broadcasted_iota(jnp.int32, (W, ROWS), 1), W)
        allowed = (key >= W - slots[0, i]) & (key <= query)
        scores = jnp.where(allowed, dot(krb[i], qt[i]), NEG)
        values = jnp.concatenate([vrb[i].T, jnp.ones((16, W), BF)], axis=0)
        soften(i, None, [scores], [values], [wb.at[i]])

    def forward(i, step):
        seen = slots[1, i]
        scores, values, keep = [], [], []
        for a in chunks_of(step):
            s = dot(kv[a, :, 0].reshape(CHUNK, HD), qt[i])
            first = lax.rem(y + a, Y) * CHUNK
            key = lax.broadcasted_iota(jnp.int32, (W, 1), 0) + first
            left = jnp.concatenate([key + lax.rem(x + OFF[n], X) * W for n in range(X)], axis=0)
            scores.append(jnp.where(left < seen, s, NEG))
            values.append(vt[a])
            keep.append(eb.at[i, a])
        soften(i, step, scores, values, keep)

    targets = ((outs, out, GW), (dqs, dq, GW), (dkrs, dkr, HD), (dvrs, dvr, HD), (None, dkp, HD), (None, dvp, HD))

    def leave_source(kind, i):
        if kind >= 4:
            return fin.at[kind - 4, i]
        return targets[kind][0].at[i]

    def leave_target(kind):
        ref, width = targets[kind][1:]
        return ref.at[:, pl.ds(pl.multiple_of(x * width, HD), width)]

    def leave(kind, d):
        return pltpu.make_async_remote_copy(
            src_ref=leave_source(kind, SLOT[d]),
            dst_ref=leave_target(kind),
            send_sem=out_ss.at[kind, d - 1],
            recv_sem=out_rs.at[kind, d - 1],
            device_id=peer(d),
            device_id_type=MESH,
        )

    def leave_own(kind):
        return pltpu.make_async_copy(leave_source(kind, 0), leave_target(kind), out_ls.at[kind])

    def go(kind, i):
        if i == 0:
            leave_own(kind).start()
        else:
            leave(kind, OFF[i]).start()

    def finish(i):
        entered(5, i)
        inverse = 1.0 / oacc[i, HD : HD + 1, :]
        attended = oacc[i, 0:HD, :] * inverse
        grads_t = natural(dob, i).T
        dot_t[i] = grads_t
        stat[i, 0:1, :] = jnp.sum(grads_t.astype(F32) * attended, axis=0, keepdims=True)
        stat[i, 1:2, :] = inverse
        turned = attended.T.astype(BF)
        for n in range(HPG):
            outs[i, :, n * HD : (n + 1) * HD] = turned[n * W : (n + 1) * W]
        go(0, i)

    def gradients(i, step, e, values):
        factor = jnp.exp2((mb[i, step] - mcur[i]) * LOG2) * stat[i, 1:2, :]
        prob = e.astype(F32) * factor
        dscore = prob * (dot(values, dot_t[i]) - stat[i, 0:1, :])
        return prob.astype(BF), dscore.astype(BF)

    def backward_window(i):
        prob, dscore = gradients(i, 5, wb[i], vrb[i])
        dvrs[i] = dot(prob, natural(dob, i)).astype(BF)
        dkrs[i] = (dot(dscore, natural(qb, i)) * SCALE).astype(BF)
        dqacc[i] = dot(krb[i].T, dscore)
        go(2, i)
        go(3, i)

    def backward(i, step, first):
        grads, queries = natural(dob, i), natural(qb, i)
        total = dqacc[i]
        for a in chunks_of(step):
            prob, dscore = gradients(i, step, eb[i, a], kv[a, :, 1].reshape(CHUNK, HD))
            dv, dk = dot(prob, grads), dot(dscore, queries)
            dvacc[a] = dv if first else dvacc[a] + dv
            dkacc[a] = dk if first else dkacc[a] + dk
            total = total + dot(kt[a], dscore)
        dqacc[i] = total

    def finish_dq(i):
        turned = (dqacc[i] * SCALE).T.astype(BF)
        for n in range(HPG):
            dqs[i, :, n * HD : (n + 1) * HD] = turned[n * W : (n + 1) * W]
        go(1, i)

    def reach(kind, direction):
        return 4 if kind == direction else 3

    def scatter(kind, direction, hop, piece):
        return pltpu.make_async_remote_copy(
            src_ref=rs_s.at[direction, kind, hop - 1, piece],
            dst_ref=rs_r.at[direction, kind, hop - 1, piece],
            send_sem=rs_ss.at[direction, kind, hop - 1, piece],
            recv_sem=rs_rs.at[direction, kind, hop - 1, piece],
            device_id=ring(direction),
            device_id_type=MESH,
        )

    def partial(kind, a, piece):
        rows = slice(piece * PIECE, (piece + 1) * PIECE)
        return dkacc[a, rows] * SCALE if kind == 0 else dvacc[a, rows]

    def arrived(kind, direction, away, piece):
        hop = reach(kind, direction) - away
        scatter(kind, direction, hop, piece).wait_recv()
        return rs_r[direction, kind, hop - 1, piece].astype(F32)

    def pass_on(kind, direction, away, piece):
        total = partial(kind, away if direction == UP else (Y - away) % Y, piece)
        if away < reach(kind, direction):
            total = total + arrived(kind, direction, away, piece)
        hop = reach(kind, direction) - away + 1
        rs_s[direction, kind, hop - 1, piece] = total.astype(BF)
        scatter(kind, direction, hop, piece).start()

    def pass_all(away, piece):
        for kind, direction in ((0, UP), (1, DOWN), (1, UP), (0, DOWN)):
            if away <= reach(kind, direction):
                pass_on(kind, direction, away, piece)

    spread(0)
    ready(0)
    for i in (1, 2, 3):
        spread(i)
    turn(0)
    forward(0, 0)
    for i in range(X):
        hop_on(1, i)
    turn(1)
    turn(7)
    forward(0, 1)
    ready(1)
    forward(1, 0)
    forward(1, 1)
    ready(2)
    forward(2, 0)
    hop_on(2, 0)
    hop_on(2, 1)
    forward(2, 1)
    hop_on(2, 2)
    hop_on(2, 3)
    turn(2)
    turn(6)
    forward(0, 2)
    forward(1, 2)
    hop_on(3, 0)
    ready(3)
    forward(3, 0)
    hop_on(3, 1)
    forward(2, 2)
    hop_on(3, 2)
    forward(3, 1)
    hop_on(3, 3)
    turn(3)
    turn(5)
    forward(3, 2)
    forward(0, 3)
    forward(1, 3)
    for i in range(X):
        hop_on(4, i)
    turn(4)
    forward(2, 3)
    forward(3, 3)
    for i in range(X):
        forward(i, 4)
    order = (3, 2, 1, 0)
    for i in order:
        finish(i)
        backward_window(i)
    for n, i in enumerate(order):
        backward(i, 4, n == 0)
    for piece in range(PIECES):
        pass_all(4, piece)
    for n, i in enumerate(order):
        backward(i, 3, n == 0)
    for piece in range(PIECES):
        pass_all(3, piece)
    for n, i in enumerate(order):
        backward(i, 2, n == 0)
        pass
    for piece in range(PIECES):
        pass_all(2, piece)
    for n, i in enumerate(order):
        backward(i, 1, n == 0)
        backward(i, 0, n == 0)
        finish_dq(i)
    for piece in range(PIECES):
        pass_all(1, piece)
    for piece in range(PIECES):
        for kind in (0, 1):
            total = partial(kind, 0, piece) + arrived(kind, UP, 0, piece) + arrived(kind, DOWN, 0, piece)
            for n in range(PIECE // W):
                fin[kind, piece * (PIECE // W) + n] = total[n * W : (n + 1) * W].astype(BF)
                go(kind + 4, piece * (PIECE // W) + n)

    for kind in range(6):
        for d in (1, 2, 3):
            enter(kind, d).wait_send()
    for hop in range(1, 5):
        for direction in (UP, DOWN):
            for i in range(X):
                gather(hop, direction, i).wait_send()
    for kind in (0, 1):
        for direction in (UP, DOWN):
            for hop in range(1, reach(kind, direction) + 1):
                for piece in range(PIECES):
                    scatter(kind, direction, hop, piece).wait_send()
    for kind in range(6):
        leave_own(kind).wait()
        for d in (1, 2, 3):
            leave(kind, d).wait()


def hand_over(*refs):
    ins, outs, held, sems = refs[:6], refs[6:12], refs[12:18], refs[18]
    first = [pltpu.make_async_copy(ins[n], held[n], sems.at[0, n]) for n in range(6)]
    second = [pltpu.make_async_copy(held[n], outs[n], sems.at[1, n]) for n in range(6)]
    for copy in first:
        copy.start()
    for n in range(6):
        first[n].wait()
        second[n].start()
    for copy in second:
        copy.wait()


def body(q_resp, k_resp, v_resp, k_prompt, v_prompt, d_out, owner, lengths, visible):
    hbm = pl.BlockSpec(memory_space=pltpu.HBM)
    smem = pl.BlockSpec(memory_space=pltpu.SMEM)
    wide = jax.ShapeDtypeStruct((W, H * HD), BF)
    narrow = jax.ShapeDtypeStruct((W, G * HD), BF)
    shapes = (wide, wide, narrow, narrow, narrow, narrow)
    dma = pltpu.SemaphoreType.DMA
    results = pl.pallas_call(
        kernel,
        out_shape=shapes,
        in_specs=[smem] * 3 + [hbm] * 6,
        out_specs=(hbm,) * 6,
        scratch_shapes=[
            pltpu.SMEM((2, X), jnp.int32),
            pltpu.VMEM((X, W, GW), BF),
            pltpu.VMEM((X, W, GW), BF),
            pltpu.VMEM((X, W, HD), BF),
            pltpu.VMEM((X, W, HD), BF),
            pltpu.VMEM((Y, X, 2, W, HD), BF),
            pltpu.VMEM((Y, HD, CHUNK), BF),
            pltpu.VMEM((Y, HD + 16, CHUNK), BF),
            pltpu.VMEM((X, HD, ROWS), BF),
            pltpu.VMEM((X, HD, ROWS), BF),
            pltpu.VMEM((X, Y, CHUNK, ROWS), BF),
            pltpu.VMEM((X, W, ROWS), BF),
            pltpu.VMEM((X, 6, 1, ROWS), F32),
            pltpu.VMEM((X, 1, ROWS), F32),
            pltpu.VMEM((X, HD + 16, ROWS), F32),
            pltpu.VMEM((X, 8, ROWS), F32),
            pltpu.VMEM((X, HD, ROWS), F32),
            pltpu.VMEM((Y, CHUNK, HD), F32),
            pltpu.VMEM((Y, CHUNK, HD), F32),
            pltpu.VMEM((X, W, GW), BF),
            pltpu.VMEM((X, W, GW), BF),
            pltpu.VMEM((X, W, HD), BF),
            pltpu.VMEM((X, W, HD), BF),
            pltpu.VMEM((2, 2, 4, PIECES, PIECE, HD), BF),
            pltpu.VMEM((2, 2, 4, PIECES, PIECE, HD), BF),
            pltpu.VMEM((2, X, W, HD), BF),
            dma((6,)), dma((6, 3)), dma((6, 3)),
            dma((4, 2, X)), dma((4, 2, X)),
            dma((6,)), dma((6, 3)), dma((6, 3)),
            dma((2, 2, 4, PIECES)), dma((2, 2, 4, PIECES)),
        ],
        compiler_params=pltpu.CompilerParams(
            collective_id=0, has_side_effects=True, vmem_limit_bytes=56 * 2**20
        ),
    )(owner, lengths, visible, q_resp, k_resp, v_resp, k_prompt, v_prompt, d_out)
    return pl.pallas_call(
        hand_over,
        out_shape=shapes,
        in_specs=[hbm] * 6,
        out_specs=(hbm,) * 6,
        scratch_shapes=[pltpu.VMEM(shape.shape, BF) for shape in shapes] + [dma((2, 6))],
    )(*results)


def solution(mesh):
    rows = P(("grp", "ctx"), None)
    in_specs = (rows,) * 6 + (P("grp"),) * 3
    return jax.shard_map(
        body, mesh=mesh, in_specs=in_specs, out_specs=(rows,) * 6, check_vma=False
    )
```

```python
import functools
import math

import jax
import jax.numpy as jnp
from jax import lax
from jax.experimental import pallas as pl
from jax.experimental.pallas import tpu as pltpu
from jax.sharding import PartitionSpec as P

H = 32
G = 4
HD = 128
HPG = H // G
GW = HPG * HD
X = 4
Y = 8
W = 64
ROWS = HPG * W
CHUNK = X * W
NEG = -1e30
SCALE = 1.0 / math.sqrt(HD)
LOG2 = SCALE * math.log2(math.e)
MESH = pl.DeviceIdType.MESH
BF = jnp.bfloat16
F32 = jnp.float32
UP, DOWN = 0, 1
PIECES = 4
PIECE = CHUNK // PIECES
OFF = (0, 1, 3, 2)
SLOT = (0, 1, 3, 2)


def dot(a, b):
    return lax.dot_general(a, b, (((1,), (0,)), ((), ())), preferred_element_type=F32)


def kernel(
    owner, lengths, visible, q, kr, vr, kp, vp, do,
    out, dq, dkp, dvp, dkr, dvr,
    slots, qb, dob, krb, vrb, kv, kt, vt, qt, dot_t, eb, wb, mb, mcur, oacc, stat,
    dqacc, dkacc, dvacc, outs, dqs, dkrs, dvrs, rs_s, rs_r, fin,
    in_ls, kv_ss, in_ss, in_rs, ag_ss, ag_rs, out_ls, out_ss, out_rs, rs_ss, rs_rs,
):
    c = lax.axis_index("ctx")
    y = c // X
    x = lax.rem(c, X)

    def at(rows, columns):
        return {"ctx": lax.rem(y + rows + Y, Y) * X + lax.rem(x + columns, X)}

    def drain(sem, kib):
        n = -(-kib // 256)
        while kib % n or kib // n % 16:
            n += 1
        ref = eb.at[0, 0:n, 0 : kib // n]
        pltpu.make_async_copy(ref, ref, sem).wait()

    def send(src, dst, send_sem, recv_sem, rows, columns):
        pltpu.make_async_remote_copy(
            src_ref=src,
            dst_ref=dst,
            send_sem=send_sem,
            recv_sem=recv_sem,
            device_id=at(rows, columns),
            device_id_type=MESH,
        ).start()

    partners = [(0, d) for d in (1, 2, 3)] + [(2, 0), (-2, 0)]
    partners += [(rows, d) for rows in (1, -1) for d in range(X)]
    barrier = pltpu.get_barrier_semaphore()
    for rows, columns in partners:
        pl.semaphore_signal(barrier, inc=1, device_id=at(rows, columns), device_id_type=MESH)

    sources = ((kp, HD), (vp, HD), (kr, HD), (vr, HD), (q, GW), (do, GW))

    def landing(kind, slot):
        if kind < 2:
            return kv.at[0, slot, kind]
        return (krb, vrb, qb, dob)[kind - 2].at[slot]

    parts = ((0, 1), (4,), (2, 3), (5,))
    part_kib = (32, 128, 32, 128)

    def enter(part, d, rows=0):
        slot = SLOT[-d % X]
        for kind in parts[part]:
            ref, width = sources[kind]
            column = pl.multiple_of(lax.rem(x + d, X) * width, HD)
            src = ref.at[:, pl.ds(column, width)]
            if part == 0:
                arrival = in_rs.at[0, slot - 1] if rows == 0 else ag_rs.at[0, slot]
                send(src, kv.at[-rows % Y, slot, kind], kv_ss, arrival, rows, d)
            else:
                send(src, landing(kind, slot), in_ss, in_rs.at[part, slot - 1], 0, d)

    def enter_own(part):
        for kind in parts[part]:
            ref, width = sources[kind]
            column = pl.multiple_of(x * width, HD)
            pltpu.make_async_copy(
                ref.at[:, pl.ds(column, width)], landing(kind, 0), in_ls.at[part]
            ).start()

    def entered(part, i):
        drain(in_ls.at[part] if i == 0 else in_rs.at[part, i - 1], part_kib[part])

    for part in range(4):
        enter_own(part)

    for i in range(X):
        holder = y * X + lax.rem(x + OFF[i], X)

        def count(j, carry, holder=holder):
            hit = owner[j] == holder
            return (
                carry[0] + jnp.where(hit, lengths[j], 0),
                carry[1] + jnp.where(hit, visible[j], 0),
            )

        length, seen = lax.fori_loop(0, Y * X, count, (jnp.int32(0), jnp.int32(0)))
        slots[0, i] = length
        slots[1, i] = seen

    pl.semaphore_wait(barrier, len(partners))
    for d in (0, 1, 3, 2):
        enter(0, d, 1)
        enter(0, d, -1)
        if d:
            enter(0, d)
    for part in (1, 2, 3):
        for d in (1, 3, 2):
            enter(part, d)

    def gather(hop, direction, i):
        sign = 1 if direction == UP else -1
        src, dst = -sign * (hop - 1) % Y, -sign * hop % Y
        if hop == 4:
            src = -sign * 2 % Y
            send(
                kv.at[src, i, direction], kv.at[4, i, direction],
                ag_ss, ag_rs.at[3, i], 2 * sign, 0,
            )
        else:
            send(kv.at[src, i], kv.at[dst, i], ag_ss, ag_rs.at[hop - 1, i], sign, 0)

    def hop_on(hop, i):
        drain(ag_rs.at[hop - 1, i], 64 if hop < 4 else 32)
        for after in {1: (2,), 2: (3, 4)}.get(hop, ()):
            gather(after, UP, i)
            gather(after, DOWN, i)

    def turn(a):
        kt[a] = kv[a, :, 0].reshape(CHUNK, HD).T
        vt[a, 0:HD, :] = kv[a, :, 1].reshape(CHUNK, HD).T
        vt[a, HD:, :] = jnp.ones((16, CHUNK), BF)

    def natural(ref, i):
        return jnp.concatenate([ref[i, :, n * HD : (n + 1) * HD] for n in range(HPG)], axis=0)

    def chunks_of(step):
        return (step,) if step in (0, 4) else (Y - step, step)

    def soften(i, step, scores, top, values_t, keep):
        if step != 0:
            before = mcur[i]
            top = jnp.maximum(top, before)
        mcur[i] = top
        mb[i, step] = top
        total = None
        for s, values, ref in zip(scores, values_t, keep):
            e = jnp.exp2((s - top) * LOG2).astype(BF)
            ref[...] = e
            term = dot(values, e)
            total = term if total is None else total + term
        if step == 0:
            oacc[i] = total
        else:
            oacc[i] = oacc[i] * jnp.exp2((before - top) * LOG2) + total

    def ready(i):
        entered(1, i)
        qt[i] = natural(qb, i).T

    def score(i, step):
        if step == 5:
            entered(2, i)
            key = lax.broadcasted_iota(jnp.int32, (W, ROWS), 0)
            query = lax.rem(lax.broadcasted_iota(jnp.int32, (W, ROWS), 1), W)
            allowed = (key >= W - slots[0, i]) & (key <= query)
            scores = [jnp.where(allowed, dot(krb[i], qt[i]), NEG)]
            values = [jnp.concatenate([vrb[i].T, jnp.ones((16, W), BF)], axis=0)]
            keep = [wb.at[i]]
        else:
            seen = slots[1, i]
            scores, values, keep = [], [], []
            for a in chunks_of(step):
                s = dot(kv[a, :, 0].reshape(CHUNK, HD), qt[i])
                first = lax.rem(y + a, Y) * CHUNK
                key = lax.broadcasted_iota(jnp.int32, (W, HD), 0) + first
                left = jnp.concatenate([key + lax.rem(x + OFF[n], X) * W for n in range(X)], axis=0)
                hide = jnp.where(left < seen, 0.0, NEG)
                scores.append(s + jnp.concatenate([hide] * (ROWS // HD), axis=1))
                values.append(vt[a])
                keep.append(eb.at[i, a])
        top = functools.reduce(
            jnp.maximum, [jnp.max(s, axis=0, keepdims=True) for s in scores]
        )
        return i, step, scores, top, values, keep

    def forward(*blocks):
        waiting = None
        for block in blocks:
            scored = score(*block)
            if waiting is not None:
                soften(*waiting)
            waiting = scored
        soften(*waiting)

    results = (
        (outs, out, GW), (dqs, dq, GW), (dkrs, dkr, HD), (dvrs, dvr, HD),
        (fin.at[0], dkp, HD), (fin.at[1], dvp, HD),
    )

    def go(kind, i):
        ref, target, width = results[kind]
        dst = target.at[:, pl.ds(pl.multiple_of(x * width, HD), width)]
        if i == 0:
            pltpu.make_async_copy(ref.at[0], dst, out_ls).start()
        else:
            send(ref.at[i], dst, out_ss, out_rs, 0, OFF[i])

    def finish(i):
        entered(3, i)
        inverse = 1.0 / oacc[i, HD : HD + 1, :]
        attended = oacc[i, 0:HD, :] * inverse
        grads_t = natural(dob, i).T
        dot_t[i] = grads_t
        stat[i, 0:1, :] = jnp.sum(grads_t.astype(F32) * attended, axis=0, keepdims=True)
        stat[i, 1:2, :] = inverse
        turned = attended.T.astype(BF)
        for n in range(HPG):
            outs[i, :, n * HD : (n + 1) * HD] = turned[n * W : (n + 1) * W]
        go(0, i)

    def gradients(i, step, e, values):
        factor = jnp.exp2((mb[i, step] - mcur[i]) * LOG2) * stat[i, 1:2, :]
        prob = e.astype(F32) * factor
        dscore = prob * (dot(values, dot_t[i]) - stat[i, 0:1, :])
        return prob.astype(BF), dscore.astype(BF)

    def backward_window(i):
        prob, dscore = gradients(i, 5, wb[i], vrb[i])
        dvrs[i] = dot(prob, natural(dob, i)).astype(BF)
        dkrs[i] = (dot(dscore, natural(qb, i)) * SCALE).astype(BF)
        dqacc[i] += dot(krb[i].T, dscore)
        go(2, i)
        go(3, i)

    def backward(i, step, first):
        grads, queries = natural(dob, i), natural(qb, i)
        total = 0.0 if step == 4 else dqacc[i]
        for a in chunks_of(step):
            prob, dscore = gradients(i, step, eb[i, a], kv[a, :, 1].reshape(CHUNK, HD))
            dv, dk = dot(prob, grads), dot(dscore, queries)
            dvacc[a] = dv if first else dvacc[a] + dv
            dkacc[a] = dk if first else dkacc[a] + dk
            total = total + dot(kt[a], dscore)
        dqacc[i] = total

    def finish_dq(i):
        turned = (dqacc[i] * SCALE).T.astype(BF)
        for n in range(HPG):
            dqs[i, :, n * HD : (n + 1) * HD] = turned[n * W : (n + 1) * W]
        go(1, i)

    def partial(kind, a, piece):
        rows = slice(piece * PIECE, (piece + 1) * PIECE)
        return dkacc[a, rows] * SCALE if kind == 0 else dvacc[a, rows]

    def pass_on(away, piece):
        if away == 4:
            for kind, sign in ((0, 1), (1, -1)):
                rs_s[3, kind, 0, piece] = partial(kind, 4, piece).astype(BF)
                send(
                    rs_s.at[3, kind, 0, piece], rs_r.at[3, kind, 0, piece],
                    rs_ss, rs_rs.at[0, piece], 2 * sign, 0,
                )
            return
        if away < 3:
            drain(rs_rs.at[2 - away, piece], (384 if away == 2 else 256) // PIECES)
        for kind in (0, 1):
            for direction in (UP, DOWN):
                sign = 1 if direction == UP else -1
                total = partial(kind, sign * away % Y, piece)
                if away < 3:
                    total = total + rs_r[away, kind, direction, piece].astype(F32)
                if away == 2 and kind == direction:
                    total = total + rs_r[3, kind, 0, piece].astype(F32)
                total = total.astype(BF)
                rs_s[away - 1, kind, direction, piece] = total
                send(
                    rs_s.at[away - 1, kind, direction, piece],
                    rs_r.at[away - 1, kind, direction, piece],
                    rs_ss, rs_rs.at[3 - away, piece], sign, 0,
                )

    def pass_out(piece):
        drain(rs_rs.at[2, piece], 256 // PIECES)
        for kind in (0, 1):
            total = partial(kind, 0, piece)
            for direction in (UP, DOWN):
                total = total + rs_r[0, kind, direction, piece].astype(F32)
            for n in range(PIECE // W):
                fin[kind, piece * (PIECE // W) + n] = total[n * W : (n + 1) * W].astype(BF)
                go(4 + kind, piece * (PIECE // W) + n)

    entered(0, 0)
    ready(0)
    hop_on(1, 0)
    entered(0, 1)
    entered(0, 2)
    hop_on(1, 1)
    hop_on(1, 2)
    entered(0, 3)
    hop_on(1, 3)
    turn(0)
    turn(1)
    turn(7)
    forward((0, 0), (0, 1))
    for i in range(X):
        hop_on(2, i)
    turn(2)
    turn(6)
    ready(1)
    forward((1, 0), (0, 2), (1, 1))
    ready(2)
    forward((2, 0), (1, 2), (2, 1), (2, 2))
    for i in range(X):
        hop_on(3, i)
    turn(3)
    turn(5)
    forward((0, 3), (1, 3), (2, 3))
    for i in range(X):
        hop_on(4, i)
    turn(4)
    ready(3)
    forward((3, 0), (0, 4), (3, 1), (1, 4), (3, 2), (2, 4), (3, 3), (3, 4))
    forward((0, 5), (1, 5), (2, 5), (3, 5))
    for i in range(X):
        finish(i)
        backward(i, 4, i == 0)
        if i == 3:
            for piece in range(PIECES):
                pass_on(4, piece)
        backward(i, 3, i == 0)
        if i == 3:
            for piece in range(PIECES):
                pass_on(3, piece)
    for i in (3, 2):
        backward_window(i)
        for step in (2, 1, 0):
            backward(i, step, i == 3)
        finish_dq(i)
    backward(1, 2, False)
    backward(0, 2, False)
    for piece in range(PIECES):
        pass_on(2, piece)
    backward_window(1)
    backward(1, 1, False)
    backward(1, 0, False)
    finish_dq(1)
    backward(0, 1, False)
    for piece in range(PIECES):
        pass_on(1, piece)
    backward_window(0)
    backward(0, 0, False)
    finish_dq(0)
    for piece in range(PIECES):
        pass_out(piece)

    drain(kv_ss, 352)
    drain(in_ss, 864)
    drain(ag_ss, 640)
    drain(rs_ss, 896)
    drain(out_ss, 960)
    drain(out_rs, 960)
    drain(out_ls, 320)


def hand_over(*refs):
    ins, outs, held, sems = refs[:6], refs[6:12], refs[12:18], refs[18]
    first = [pltpu.make_async_copy(ins[n], held[n], sems.at[0, n]) for n in range(6)]
    second = [pltpu.make_async_copy(held[n], outs[n], sems.at[1, n]) for n in range(6)]
    for copy in first:
        copy.start()
    for n in range(6):
        first[n].wait()
        second[n].start()
    for copy in second:
        copy.wait()


def body(q_resp, k_resp, v_resp, k_prompt, v_prompt, d_out, owner, lengths, visible):
    hbm = pl.BlockSpec(memory_space=pltpu.HBM)
    smem = pl.BlockSpec(memory_space=pltpu.SMEM)
    wide = jax.ShapeDtypeStruct((W, H * HD), BF)
    narrow = jax.ShapeDtypeStruct((W, G * HD), BF)
    shapes = (wide, wide, narrow, narrow, narrow, narrow)
    dma = pltpu.SemaphoreType.DMA
    results = pl.pallas_call(
        kernel,
        out_shape=shapes,
        in_specs=[smem] * 3 + [hbm] * 6,
        out_specs=(hbm,) * 6,
        scratch_shapes=[
            pltpu.SMEM((2, X), jnp.int32),
            pltpu.VMEM((X, W, GW), BF),
            pltpu.VMEM((X, W, GW), BF),
            pltpu.VMEM((X, W, HD), BF),
            pltpu.VMEM((X, W, HD), BF),
            pltpu.VMEM((Y, X, 2, W, HD), BF),
            pltpu.VMEM((Y, HD, CHUNK), BF),
            pltpu.VMEM((Y, HD + 16, CHUNK), BF),
            pltpu.VMEM((X, HD, ROWS), BF),
            pltpu.VMEM((X, HD, ROWS), BF),
            pltpu.VMEM((X, Y, CHUNK, ROWS), BF),
            pltpu.VMEM((X, W, ROWS), BF),
            pltpu.VMEM((X, 6, 1, ROWS), F32),
            pltpu.VMEM((X, 1, ROWS), F32),
            pltpu.VMEM((X, HD + 16, ROWS), F32),
            pltpu.VMEM((X, 8, ROWS), F32),
            pltpu.VMEM((X, HD, ROWS), F32),
            pltpu.VMEM((Y, CHUNK, HD), F32),
            pltpu.VMEM((Y, CHUNK, HD), F32),
            pltpu.VMEM((X, W, GW), BF),
            pltpu.VMEM((X, W, GW), BF),
            pltpu.VMEM((X, W, HD), BF),
            pltpu.VMEM((X, W, HD), BF),
            pltpu.VMEM((4, 2, 2, PIECES, PIECE, HD), BF),
            pltpu.VMEM((4, 2, 2, PIECES, PIECE, HD), BF),
            pltpu.VMEM((2, X, W, HD), BF),
            dma((4,)), dma, dma, dma((4, 3)),
            dma, dma((4, X)),
            dma, dma, dma,
            dma, dma((3, PIECES)),
        ],
        compiler_params=pltpu.CompilerParams(
            collective_id=0, has_side_effects=True, vmem_limit_bytes=56 * 2**20
        ),
    )(owner, lengths, visible, q_resp, k_resp, v_resp, k_prompt, v_prompt, d_out)
    return pl.pallas_call(
        hand_over,
        out_shape=shapes,
        in_specs=[hbm] * 6,
        out_specs=(hbm,) * 6,
        scratch_shapes=[pltpu.VMEM(shape.shape, BF) for shape in shapes] + [dma((2, 6))],
    )(*results)


def solution(mesh):
    rows = P(("grp", "ctx"), None)
    in_specs = (rows,) * 6 + (P("grp"),) * 3
    return jax.shard_map(
        body, mesh=mesh, in_specs=in_specs, out_specs=(rows,) * 6, check_vma=False
    )
```

```python
import functools
import math

import jax
import jax.numpy as jnp
from jax import lax
from jax.experimental import pallas as pl
from jax.experimental.pallas import tpu as pltpu
from jax.sharding import PartitionSpec as P

H = 32
G = 4
HD = 128
HPG = H // G
GW = HPG * HD
X = 4
Y = 8
W = 64
ROWS = HPG * W
CHUNK = X * W
NEG = -1e30
SCALE = 1.0 / math.sqrt(HD)
LOG2 = SCALE * math.log2(math.e)
MESH = pl.DeviceIdType.MESH
BF = jnp.bfloat16
F32 = jnp.float32
UP, DOWN = 0, 1
PIECES = 4
PIECE = CHUNK // PIECES
OFF = (0, 1, 3, 2)
SLOT = (0, 1, 3, 2)


def dot(a, b):
    return lax.dot_general(a, b, (((1,), (0,)), ((), ())), preferred_element_type=F32)


def kernel(
    owner, lengths, visible, q, kr, vr, kp, vp, do,
    out, dq, dkp, dvp, dkr, dvr,
    slots, qb, dob, krb, vrb, kv, kt, vt, qt, dot_t, eb, wb, mb, mcur, oacc, stat,
    dqacc, dkacc, dvacc, outs, dqs, dkrs, dvrs, rs_s, rs_r, tail_s, tail_r, fin,
    in_ls, kv_ss, in_ss, in_rs, ag_ss, ag_rs, out_ls, out_ss, out_rs, rs_ss, rs_rs, tail_ss, tail_rs,
):
    c = lax.axis_index("ctx")
    y = c // X
    x = lax.rem(c, X)

    def at(rows, columns):
        return {"ctx": lax.rem(y + rows + Y, Y) * X + lax.rem(x + columns, X)}

    def drain(sem, kib):
        n = -(-kib // 256)
        while kib % n or kib // n % 16:
            n += 1
        ref = eb.at[0, 0:n, 0 : kib // n]
        pltpu.make_async_copy(ref, ref, sem).wait()

    def send(src, dst, send_sem, recv_sem, rows, columns):
        pltpu.make_async_remote_copy(
            src_ref=src,
            dst_ref=dst,
            send_sem=send_sem,
            recv_sem=recv_sem,
            device_id=at(rows, columns),
            device_id_type=MESH,
        ).start()

    partners = [(0, d) for d in (1, 2, 3)] + [(2, 0), (-2, 0)]
    partners += [(rows, d) for rows in (1, -1) for d in range(X)]
    barrier = pltpu.get_barrier_semaphore()
    for rows, columns in partners:
        pl.semaphore_signal(barrier, inc=1, device_id=at(rows, columns), device_id_type=MESH)

    sources = ((kp, HD), (vp, HD), (kr, HD), (vr, HD), (q, GW), (do, GW))

    def landing(kind, slot):
        if kind < 2:
            return kv.at[0, slot, kind]
        return (krb, vrb, qb, dob)[kind - 2].at[slot]

    parts = ((0, 1), (4,), (2, 3), (5,))
    part_kib = (32, 128, 32, 128)

    def enter(part, d, rows=0):
        slot = SLOT[-d % X]
        for kind in parts[part]:
            ref, width = sources[kind]
            column = pl.multiple_of(lax.rem(x + d, X) * width, HD)
            src = ref.at[:, pl.ds(column, width)]
            if part == 0:
                arrival = in_rs.at[0, slot - 1] if rows == 0 else ag_rs.at[0, slot]
                send(src, kv.at[-rows % Y, slot, kind], kv_ss, arrival, rows, d)
            else:
                send(src, landing(kind, slot), in_ss, in_rs.at[part, slot - 1], 0, d)

    def enter_own(part):
        for kind in parts[part]:
            ref, width = sources[kind]
            column = pl.multiple_of(x * width, HD)
            pltpu.make_async_copy(
                ref.at[:, pl.ds(column, width)], landing(kind, 0), in_ls.at[part]
            ).start()

    def entered(part, i):
        drain(in_ls.at[part] if i == 0 else in_rs.at[part, i - 1], part_kib[part])

    for part in range(4):
        enter_own(part)

    for i in range(X):
        holder = y * X + lax.rem(x + OFF[i], X)

        def count(j, carry, holder=holder):
            hit = owner[j] == holder
            return (
                carry[0] + jnp.where(hit, lengths[j], 0),
                carry[1] + jnp.where(hit, visible[j], 0),
            )

        length, seen = lax.fori_loop(0, Y * X, count, (jnp.int32(0), jnp.int32(0)))
        slots[0, i] = length
        slots[1, i] = seen

    pl.semaphore_wait(barrier, len(partners))
    for d in (0, 1, 3, 2):
        enter(0, d, 1)
        enter(0, d, -1)
        if d:
            enter(0, d)
    for part in (1, 2, 3):
        for d in (1, 3, 2):
            enter(part, d)

    def gather(hop, direction, i):
        sign = 1 if direction == UP else -1
        src, dst = -sign * (hop - 1) % Y, -sign * hop % Y
        if hop == 4:
            src = -sign * 2 % Y
            send(
                kv.at[src, i, direction], kv.at[4, i, direction],
                ag_ss, ag_rs.at[3, i], 2 * sign, 0,
            )
        else:
            send(kv.at[src, i], kv.at[dst, i], ag_ss, ag_rs.at[hop - 1, i], sign, 0)

    def hop_on(hop, i):
        drain(ag_rs.at[hop - 1, i], 64 if hop < 4 else 32)
        for after in {1: (2,), 2: (3, 4)}.get(hop, ()):
            gather(after, UP, i)
            gather(after, DOWN, i)

    def turn(a):
        kt[a] = kv[a, :, 0].reshape(CHUNK, HD).T
        vt[a, 0:HD, :] = kv[a, :, 1].reshape(CHUNK, HD).T
        vt[a, HD:, :] = jnp.ones((16, CHUNK), BF)

    def natural(ref, i):
        return jnp.concatenate([ref[i, :, n * HD : (n + 1) * HD] for n in range(HPG)], axis=0)

    def chunks_of(step):
        return (step,) if step in (0, 4) else (Y - step, step)

    def soften(i, step, scores, top, values_t, keep):
        if step != 0:
            before = mcur[i]
            top = jnp.maximum(top, before)
        mcur[i] = top
        mb[i, step] = top
        total = None
        for s, values, ref in zip(scores, values_t, keep):
            e = jnp.exp2((s - top) * LOG2).astype(BF)
            ref[...] = e
            term = dot(values, e)
            total = term if total is None else total + term
        if step == 0:
            oacc[i] = total
        else:
            oacc[i] = oacc[i] * jnp.exp2((before - top) * LOG2) + total

    def ready(i):
        entered(1, i)
        qt[i] = natural(qb, i).T

    def score(i, step):
        if step == 5:
            entered(2, i)
            key = lax.broadcasted_iota(jnp.int32, (W, ROWS), 0)
            query = lax.rem(lax.broadcasted_iota(jnp.int32, (W, ROWS), 1), W)
            allowed = (key >= W - slots[0, i]) & (key <= query)
            scores = [jnp.where(allowed, dot(krb[i], qt[i]), NEG)]
            values = [jnp.concatenate([vrb[i].T, jnp.ones((16, W), BF)], axis=0)]
            keep = [wb.at[i]]
        else:
            seen = slots[1, i]
            scores, values, keep = [], [], []
            for a in chunks_of(step):
                s = dot(kv[a, :, 0].reshape(CHUNK, HD), qt[i])
                first = lax.rem(y + a, Y) * CHUNK
                key = lax.broadcasted_iota(jnp.int32, (W, HD), 0) + first
                left = jnp.concatenate([key + lax.rem(x + OFF[n], X) * W for n in range(X)], axis=0)
                hide = jnp.where(left < seen, 0.0, NEG)
                scores.append(s + jnp.concatenate([hide] * (ROWS // HD), axis=1))
                values.append(vt[a])
                keep.append(eb.at[i, a])
        top = functools.reduce(
            jnp.maximum, [jnp.max(s, axis=0, keepdims=True) for s in scores]
        )
        return i, step, scores, top, values, keep

    def forward(*blocks):
        waiting = None
        for block in blocks:
            scored = score(*block)
            if waiting is not None:
                soften(*waiting)
            waiting = scored
        soften(*waiting)

    results = ((outs, out, GW), (dqs, dq, GW), (dkrs, dkr, HD), (dvrs, dvr, HD))

    def go(kind, i):
        ref, target, width = results[kind]
        dst = target.at[:, pl.ds(pl.multiple_of(x * width, HD), width)]
        if i == 0:
            pltpu.make_async_copy(ref.at[0], dst, out_ls).start()
        else:
            send(ref.at[i], dst, out_ss, out_rs, 0, OFF[i])

    def finish(i):
        entered(3, i)
        inverse = 1.0 / oacc[i, HD : HD + 1, :]
        attended = oacc[i, 0:HD, :] * inverse
        grads_t = natural(dob, i).T
        dot_t[i] = grads_t
        stat[i, 0:1, :] = jnp.sum(grads_t.astype(F32) * attended, axis=0, keepdims=True)
        stat[i, 1:2, :] = inverse
        turned = attended.T.astype(BF)
        for n in range(HPG):
            outs[i, :, n * HD : (n + 1) * HD] = turned[n * W : (n + 1) * W]
        go(0, i)

    def gradients(i, step, e, values):
        factor = jnp.exp2((mb[i, step] - mcur[i]) * LOG2) * stat[i, 1:2, :]
        prob = e.astype(F32) * factor
        dscore = prob * (dot(values, dot_t[i]) - stat[i, 0:1, :])
        return prob.astype(BF), dscore.astype(BF)

    def backward_window(i):
        prob, dscore = gradients(i, 5, wb[i], vrb[i])
        dvrs[i] = dot(prob, natural(dob, i)).astype(BF)
        dkrs[i] = (dot(dscore, natural(qb, i)) * SCALE).astype(BF)
        dqacc[i] += dot(krb[i].T, dscore)
        go(2, i)
        go(3, i)

    def backward(i, step, first):
        grads, queries = natural(dob, i), natural(qb, i)
        total = 0.0 if step == 4 else dqacc[i]
        for a in chunks_of(step):
            prob, dscore = gradients(i, step, eb[i, a], kv[a, :, 1].reshape(CHUNK, HD))
            dv, dk = dot(prob, grads), dot(dscore, queries)
            dvacc[a] = dv if first else dvacc[a] + dv
            dkacc[a] = dk if first else dkacc[a] + dk
            total = total + dot(kt[a], dscore)
        dqacc[i] = total

    def finish_dq(i):
        turned = (dqacc[i] * SCALE).T.astype(BF)
        for n in range(HPG):
            dqs[i, :, n * HD : (n + 1) * HD] = turned[n * W : (n + 1) * W]
        go(1, i)

    def partial(kind, a, piece):
        rows = slice(piece * PIECE, (piece + 1) * PIECE)
        return dkacc[a, rows] * SCALE if kind == 0 else dvacc[a, rows]

    def pass_on(away, piece):
        if away == 4:
            for kind, sign in ((0, 1), (1, -1)):
                rs_s[3, kind, 0, piece] = partial(kind, 4, piece).astype(BF)
                send(
                    rs_s.at[3, kind, 0, piece], rs_r.at[2, kind, 0, piece],
                    rs_ss, rs_rs.at[0, piece], 2 * sign, 0,
                )
            return
        if away < 3:
            drain(rs_rs.at[2 - away, piece], (384 if away == 2 else 256) // PIECES)
        for kind in (0, 1):
            for direction in (UP, DOWN):
                sign = 1 if direction == UP else -1
                total = partial(kind, sign * away % Y, piece)
                if away < 3:
                    total = total + rs_r[away - 1, kind, direction, piece].astype(F32)
                if away == 2 and kind == direction:
                    total = total + rs_r[2, kind, 0, piece].astype(F32)
                total = total.astype(BF)
                if away == 1:
                    leave_sum(kind, 1 + direction, piece, total)
                    continue
                rs_s[away - 1, kind, direction, piece] = total
                send(
                    rs_s.at[away - 1, kind, direction, piece],
                    rs_r.at[away - 2, kind, direction, piece],
                    rs_ss, rs_rs.at[3 - away, piece], sign, 0,
                )

    def leave_sum(kind, way, piece, total):
        for n in range(PIECE // W):
            i = piece * (PIECE // W) + n
            tail_s[way, kind, i] = total[n * W : (n + 1) * W]
            if way > 0 or i > 0:
                send(
                    tail_s.at[way, kind, i], tail_r.at[way, kind, SLOT[-OFF[i] % X]],
                    tail_ss, tail_rs, (0, 1, -1)[way], OFF[i],
                )

    entered(0, 0)
    ready(0)
    hop_on(1, 0)
    entered(0, 1)
    entered(0, 2)
    hop_on(1, 1)
    hop_on(1, 2)
    entered(0, 3)
    hop_on(1, 3)
    turn(0)
    turn(1)
    turn(7)
    forward((0, 0), (0, 1))
    hop_on(2, 0)
    ready(1)
    forward((1, 0))
    hop_on(2, 1)
    hop_on(2, 2)
    forward((1, 1))
    hop_on(2, 3)
    turn(2)
    turn(6)
    ready(2)
    forward((0, 2), (2, 0), (1, 2), (2, 1), (2, 2))
    ready(3)
    forward((3, 0), (3, 1), (3, 2), (0, 5), (1, 5), (2, 5), (3, 5))
    for i in range(X):
        hop_on(3, i)
    turn(3)
    turn(5)
    forward((0, 3), (1, 3), (2, 3), (3, 3))
    for i in range(X):
        hop_on(4, i)
    turn(4)
    forward((0, 4), (1, 4), (2, 4), (3, 4))
    for i in range(X):
        finish(i)
        backward(i, 4, i == 0)
        if i == 3:
            for piece in range(PIECES):
                pass_on(4, piece)
        backward(i, 3, i == 0)
        if i == 3:
            for piece in range(PIECES):
                pass_on(3, piece)
    for i in (3, 2, 1, 0):
        backward(i, 2, i == 3)
    backward_window(3)
    backward(3, 1, True)
    backward(3, 0, True)
    finish_dq(3)
    for piece in range(PIECES):
        pass_on(2, piece)
        i = 2 - piece * 2 // PIECES
        if piece % 2 == 0:
            backward_window(i)
            backward(i, 1, False)
        else:
            backward(i, 0, False)
            finish_dq(i)
    backward_window(0)
    backward(0, 1, False)
    backward(0, 0, False)
    for piece in range(PIECES):
        for kind in (0, 1):
            leave_sum(kind, 0, piece, partial(kind, 0, piece).astype(BF))
    finish_dq(0)
    for piece in range(PIECES):
        pass_on(1, piece)
    drain(tail_rs, 352)
    for kind, target in ((0, dkp), (1, dvp)):
        for i in range(X):
            own = tail_s[0, kind, 0] if i == 0 else tail_r[0, kind, i]
            total = own.astype(F32) + tail_r[1, kind, i].astype(F32) + tail_r[2, kind, i].astype(F32)
            fin[kind, i] = total.astype(BF)
            column = pl.multiple_of(lax.rem(x + OFF[i], X) * HD, HD)
            pltpu.make_async_copy(fin.at[kind, i], target.at[:, pl.ds(column, HD)], out_ls).start()

    drain(kv_ss, 352)
    drain(in_ss, 864)
    drain(ag_ss, 640)
    drain(rs_ss, 640)
    drain(tail_ss, 352)
    drain(out_ss, 864)
    drain(out_rs, 864)
    drain(out_ls, 416)


def hand_over(*refs):
    ins, outs, held, sems = refs[:6], refs[6:12], refs[12:18], refs[18]
    first = [pltpu.make_async_copy(ins[n], held[n], sems.at[0, n]) for n in range(6)]
    second = [pltpu.make_async_copy(held[n], outs[n], sems.at[1, n]) for n in range(6)]
    for copy in first:
        copy.start()
    for n in range(6):
        first[n].wait()
        second[n].start()
    for copy in second:
        copy.wait()


def body(q_resp, k_resp, v_resp, k_prompt, v_prompt, d_out, owner, lengths, visible):
    hbm = pl.BlockSpec(memory_space=pltpu.HBM)
    smem = pl.BlockSpec(memory_space=pltpu.SMEM)
    wide = jax.ShapeDtypeStruct((W, H * HD), BF)
    narrow = jax.ShapeDtypeStruct((W, G * HD), BF)
    shapes = (wide, wide, narrow, narrow, narrow, narrow)
    dma = pltpu.SemaphoreType.DMA
    results = pl.pallas_call(
        kernel,
        out_shape=shapes,
        in_specs=[smem] * 3 + [hbm] * 6,
        out_specs=(hbm,) * 6,
        scratch_shapes=[
            pltpu.SMEM((2, X), jnp.int32),
            pltpu.VMEM((X, W, GW), BF),
            pltpu.VMEM((X, W, GW), BF),
            pltpu.VMEM((X, W, HD), BF),
            pltpu.VMEM((X, W, HD), BF),
            pltpu.VMEM((Y, X, 2, W, HD), BF),
            pltpu.VMEM((Y, HD, CHUNK), BF),
            pltpu.VMEM((Y, HD + 16, CHUNK), BF),
            pltpu.VMEM((X, HD, ROWS), BF),
            pltpu.VMEM((X, HD, ROWS), BF),
            pltpu.VMEM((X, Y, CHUNK, ROWS), BF),
            pltpu.VMEM((X, W, ROWS), BF),
            pltpu.VMEM((X, 6, 1, ROWS), F32),
            pltpu.VMEM((X, 1, ROWS), F32),
            pltpu.VMEM((X, HD + 16, ROWS), F32),
            pltpu.VMEM((X, 8, ROWS), F32),
            pltpu.VMEM((X, HD, ROWS), F32),
            pltpu.VMEM((Y, CHUNK, HD), F32),
            pltpu.VMEM((Y, CHUNK, HD), F32),
            pltpu.VMEM((X, W, GW), BF),
            pltpu.VMEM((X, W, GW), BF),
            pltpu.VMEM((X, W, HD), BF),
            pltpu.VMEM((X, W, HD), BF),
            pltpu.VMEM((4, 2, 2, PIECES, PIECE, HD), BF),
            pltpu.VMEM((3, 2, 2, PIECES, PIECE, HD), BF),
            pltpu.VMEM((3, 2, X, W, HD), BF),
            pltpu.VMEM((3, 2, X, W, HD), BF),
            pltpu.VMEM((2, X, W, HD), BF),
            dma((4,)), dma, dma, dma((4, 3)),
            dma, dma((4, X)),
            dma, dma, dma,
            dma, dma((2, PIECES)),
            dma, dma,
        ],
        compiler_params=pltpu.CompilerParams(
            collective_id=0, has_side_effects=True, vmem_limit_bytes=56 * 2**20
        ),
    )(owner, lengths, visible, q_resp, k_resp, v_resp, k_prompt, v_prompt, d_out)
    return pl.pallas_call(
        hand_over,
        out_shape=shapes,
        in_specs=[hbm] * 6,
        out_specs=(hbm,) * 6,
        scratch_shapes=[pltpu.VMEM(shape.shape, BF) for shape in shapes] + [dma((2, 6))],
    )(*results)


def solution(mesh):
    rows = P(("grp", "ctx"), None)
    in_specs = (rows,) * 6 + (P("grp"),) * 3
    return jax.shard_map(
        body, mesh=mesh, in_specs=in_specs, out_specs=(rows,) * 6, check_vma=False
    )
```

```python
import functools
import math

import jax
import jax.numpy as jnp
from jax import lax
from jax.experimental import pallas as pl
from jax.experimental.pallas import tpu as pltpu
from jax.sharding import PartitionSpec as P

H = 32
G = 4
HD = 128
HPG = H // G
GW = HPG * HD
X = 4
Y = 8
W = 64
ROWS = HPG * W
CHUNK = X * W
NEG = -1e30
SCALE = 1.0 / math.sqrt(HD)
LOG2 = SCALE * math.log2(math.e)
MESH = pl.DeviceIdType.MESH
BF = jnp.bfloat16
F32 = jnp.float32
UP, DOWN = 0, 1
PIECES = 4
PIECE = CHUNK // PIECES
OFF = (0, 1, 3, 2)
SLOT = (0, 1, 3, 2)


def dot(a, b):
    return lax.dot_general(a, b, (((1,), (0,)), ((), ())), preferred_element_type=F32)


def kernel(
    owner, lengths, visible, q, kr, vr, kp, vp, do,
    out, dq, dkp, dvp, dkr, dvr,
    slots, qb, dob, krb, vrb, kv, kt, vt, qt, dot_t, eb, wb, mb, mcur, oacc, stat,
    dqacc, dkacc, dvacc, outs, dqs, dkrs, dvrs, rs_s, rs_r, tail_s, tail_r, fin,
    in_ls, kv_ss, in_ss, in_rs, ag_ss, ag_rs, out_ls, out_ss, out_rs, rs_ss, rs_rs, tail_ss, tail_rs,
):
    c = lax.axis_index("ctx")
    y = c // X
    x = lax.rem(c, X)

    def at(rows, columns):
        return {"ctx": lax.rem(y + rows + Y, Y) * X + lax.rem(x + columns, X)}

    def drain(sem, kib):
        n = -(-kib // 256)
        while kib % n or kib // n % 16:
            n += 1
        ref = eb.at[0, 0:n, 0 : kib // n]
        pltpu.make_async_copy(ref, ref, sem).wait()

    def send(src, dst, send_sem, recv_sem, rows, columns):
        pltpu.make_async_remote_copy(
            src_ref=src,
            dst_ref=dst,
            send_sem=send_sem,
            recv_sem=recv_sem,
            device_id=at(rows, columns),
            device_id_type=MESH,
        ).start()

    partners = [(0, d) for d in (1, 2, 3)] + [(2, 0), (-2, 0)]
    partners += [(rows, d) for rows in (1, -1) for d in range(X)]
    barrier = pltpu.get_barrier_semaphore()
    for rows, columns in partners:
        pl.semaphore_signal(barrier, inc=1, device_id=at(rows, columns), device_id_type=MESH)

    sources = ((kp, HD), (vp, HD), (kr, HD), (vr, HD), (q, GW), (do, GW))

    def landing(kind, slot):
        if kind < 2:
            return kv.at[0, slot, kind]
        return (krb, vrb, qb, dob)[kind - 2].at[slot]

    parts = ((0, 1), (4,), (2, 3), (5,))
    part_kib = (32, 128, 32, 128)

    def enter(part, d, rows=0):
        slot = SLOT[-d % X]
        for kind in parts[part]:
            ref, width = sources[kind]
            column = pl.multiple_of(lax.rem(x + d, X) * width, HD)
            src = ref.at[:, pl.ds(column, width)]
            if part == 0:
                arrival = in_rs.at[0, slot - 1] if rows == 0 else ag_rs.at[0, slot, (1 - rows) // 2]
                send(src, kv.at[-rows % Y, slot, kind], kv_ss, arrival, rows, d)
            else:
                send(src, landing(kind, slot), in_ss, in_rs.at[part, slot - 1], 0, d)

    def enter_own(part):
        for kind in parts[part]:
            ref, width = sources[kind]
            column = pl.multiple_of(x * width, HD)
            pltpu.make_async_copy(
                ref.at[:, pl.ds(column, width)], landing(kind, 0), in_ls.at[part]
            ).start()

    def entered(part, i):
        drain(in_ls.at[part] if i == 0 else in_rs.at[part, i - 1], part_kib[part])

    for part in range(4):
        enter_own(part)

    for i in range(X):
        holder = y * X + lax.rem(x + OFF[i], X)

        def count(j, carry, holder=holder):
            hit = owner[j] == holder
            return (
                carry[0] + jnp.where(hit, lengths[j], 0),
                carry[1] + jnp.where(hit, visible[j], 0),
            )

        length, seen = lax.fori_loop(0, Y * X, count, (jnp.int32(0), jnp.int32(0)))
        slots[0, i] = length
        slots[1, i] = seen

    pl.semaphore_wait(barrier, len(partners))
    for d in (0, 1, 3, 2):
        enter(0, d, 1)
        enter(0, d, -1)
        if d:
            enter(0, d)
    for part in (1, 2, 3):
        for d in (1, 3, 2):
            enter(part, d)

    def gather(hop, direction, i):
        sign = 1 if direction == UP else -1
        src, dst = -sign * (hop - 1) % Y, -sign * hop % Y
        if hop == 4:
            src = -sign * 2 % Y
            send(
                kv.at[src, i, direction], kv.at[4, i, direction],
                ag_ss, ag_rs.at[3, i, direction], 2 * sign, 0,
            )
        else:
            send(kv.at[src, i], kv.at[dst, i], ag_ss, ag_rs.at[hop - 1, i, direction], sign, 0)

    def hop_on(hop, i):
        for direction in (UP, DOWN):
            drain(ag_rs.at[hop - 1, i, direction], 32 if hop < 4 else 16)
            for after in {1: (2,), 2: (3, 4)}.get(hop, ()):
                gather(after, direction, i)

    def turn(a):
        kt[a] = kv[a, :, 0].reshape(CHUNK, HD).T
        vt[a, 0:HD, :] = kv[a, :, 1].reshape(CHUNK, HD).T
        vt[a, HD:, :] = jnp.ones((16, CHUNK), BF)

    def natural(ref, i):
        return jnp.concatenate([ref[i, :, n * HD : (n + 1) * HD] for n in range(HPG)], axis=0)

    def chunks_of(step):
        return (step,) if step in (0, 4) else (Y - step, step)

    def soften(i, step, scores, top, values_t, keep):
        if step != 0:
            before = mcur[i]
            top = jnp.maximum(top, before)
        mcur[i] = top
        mb[i, step] = top
        total = None
        for s, values, ref in zip(scores, values_t, keep):
            e = jnp.exp2((s - top) * LOG2).astype(BF)
            ref[...] = e
            term = dot(values, e)
            total = term if total is None else total + term
        if step == 0:
            oacc[i] = total
        else:
            oacc[i] = oacc[i] * jnp.exp2((before - top) * LOG2) + total

    def ready(i):
        entered(1, i)
        qt[i] = natural(qb, i).T

    def score(i, step):
        if step == 5:
            entered(2, i)
            key = lax.broadcasted_iota(jnp.int32, (W, ROWS), 0)
            query = lax.rem(lax.broadcasted_iota(jnp.int32, (W, ROWS), 1), W)
            allowed = (key >= W - slots[0, i]) & (key <= query)
            scores = [jnp.where(allowed, dot(krb[i], qt[i]), NEG)]
            values = [jnp.concatenate([vrb[i].T, jnp.ones((16, W), BF)], axis=0)]
            keep = [wb.at[i]]
        else:
            seen = slots[1, i]
            scores, values, keep = [], [], []
            for a in chunks_of(step):
                s = dot(kv[a, :, 0].reshape(CHUNK, HD), qt[i])
                first = lax.rem(y + a, Y) * CHUNK
                key = lax.broadcasted_iota(jnp.int32, (W, HD), 0) + first
                left = jnp.concatenate([key + lax.rem(x + OFF[n], X) * W for n in range(X)], axis=0)
                hide = jnp.where(left < seen, 0.0, NEG)
                scores.append(s + jnp.concatenate([hide] * (ROWS // HD), axis=1))
                values.append(vt[a])
                keep.append(eb.at[i, a])
        top = functools.reduce(
            jnp.maximum, [jnp.max(s, axis=0, keepdims=True) for s in scores]
        )
        return i, step, scores, top, values, keep

    def forward(*blocks):
        waiting = None
        for block in blocks:
            scored = score(*block)
            if waiting is not None:
                soften(*waiting)
            waiting = scored
        soften(*waiting)

    results = ((outs, out, GW), (dqs, dq, GW), (dkrs, dkr, HD), (dvrs, dvr, HD))

    def go(kind, i):
        ref, target, width = results[kind]
        dst = target.at[:, pl.ds(pl.multiple_of(x * width, HD), width)]
        if i == 0:
            pltpu.make_async_copy(ref.at[0], dst, out_ls).start()
        else:
            send(ref.at[i], dst, out_ss, out_rs, 0, OFF[i])

    def finish(i):
        entered(3, i)
        inverse = 1.0 / oacc[i, HD : HD + 1, :]
        attended = oacc[i, 0:HD, :] * inverse
        grads_t = natural(dob, i).T
        dot_t[i] = grads_t
        stat[i, 0:1, :] = jnp.sum(grads_t.astype(F32) * attended, axis=0, keepdims=True)
        stat[i, 1:2, :] = inverse
        turned = attended.T.astype(BF)
        for n in range(HPG):
            outs[i, :, n * HD : (n + 1) * HD] = turned[n * W : (n + 1) * W]
        go(0, i)

    def gradients(i, step, e, values):
        factor = jnp.exp2((mb[i, step] - mcur[i]) * LOG2) * stat[i, 1:2, :]
        prob = e.astype(F32) * factor
        dscore = prob * (dot(values, dot_t[i]) - stat[i, 0:1, :])
        return prob.astype(BF), dscore.astype(BF)

    def backward_window(i):
        prob, dscore = gradients(i, 5, wb[i], vrb[i])
        dvrs[i] = dot(prob, natural(dob, i)).astype(BF)
        dkrs[i] = (dot(dscore, natural(qb, i)) * SCALE).astype(BF)
        dqacc[i] += dot(krb[i].T, dscore)
        go(2, i)
        go(3, i)

    def backward(i, step, first):
        grads, queries = natural(dob, i), natural(qb, i)
        total = 0.0 if step == 4 else dqacc[i]
        for a in chunks_of(step):
            prob, dscore = gradients(i, step, eb[i, a], kv[a, :, 1].reshape(CHUNK, HD))
            dv, dk = dot(prob, grads), dot(dscore, queries)
            dvacc[a] = dv if first else dvacc[a] + dv
            dkacc[a] = dk if first else dkacc[a] + dk
            total = total + dot(kt[a], dscore)
        dqacc[i] = total

    def finish_dq(i):
        turned = (dqacc[i] * SCALE).T.astype(BF)
        for n in range(HPG):
            dqs[i, :, n * HD : (n + 1) * HD] = turned[n * W : (n + 1) * W]
        go(1, i)

    def partial(kind, a, piece):
        rows = slice(piece * PIECE, (piece + 1) * PIECE)
        return dkacc[a, rows] * SCALE if kind == 0 else dvacc[a, rows]

    def pass_on(away, piece):
        if away == 4:
            for kind, sign in ((0, 1), (1, -1)):
                rs_s[3, kind, 0, piece] = partial(kind, 4, piece).astype(BF)
                send(
                    rs_s.at[3, kind, 0, piece], rs_r.at[2, kind, 0, piece],
                    rs_ss, rs_rs.at[0, piece, kind], 2 * sign, 0,
                )
            return
        for direction in (UP, DOWN):
            if away < 3:
                drain(rs_rs.at[2 - away, piece, direction], (192 if away == 2 else 128) // PIECES)
            for kind in (0, 1):
                sign = 1 if direction == UP else -1
                total = partial(kind, sign * away % Y, piece)
                if away < 3:
                    total = total + rs_r[away - 1, kind, direction, piece].astype(F32)
                if away == 2 and kind == direction:
                    total = total + rs_r[2, kind, 0, piece].astype(F32)
                total = total.astype(BF)
                if away == 1:
                    leave_sum(kind, 1 + direction, piece, total)
                    continue
                rs_s[away - 1, kind, direction, piece] = total
                send(
                    rs_s.at[away - 1, kind, direction, piece],
                    rs_r.at[away - 2, kind, direction, piece],
                    rs_ss, rs_rs.at[3 - away, piece, direction], sign, 0,
                )

    def leave_sum(kind, way, piece, total):
        for n in range(PIECE // W):
            i = piece * (PIECE // W) + n
            tail_s[way, kind, i] = total[n * W : (n + 1) * W]
            if way > 0 or i > 0:
                send(
                    tail_s.at[way, kind, i], tail_r.at[way, kind, SLOT[-OFF[i] % X]],
                    tail_ss, tail_rs, (0, 1, -1)[way], OFF[i],
                )

    entered(0, 0)
    ready(0)
    hop_on(1, 0)
    entered(0, 1)
    entered(0, 2)
    hop_on(1, 1)
    hop_on(1, 2)
    entered(0, 3)
    hop_on(1, 3)
    turn(0)
    turn(1)
    turn(7)
    forward((0, 0), (0, 1))
    hop_on(2, 0)
    ready(1)
    forward((1, 0))
    hop_on(2, 1)
    hop_on(2, 2)
    forward((1, 1))
    hop_on(2, 3)
    turn(2)
    turn(6)
    ready(2)
    forward((0, 2), (2, 0), (1, 2), (2, 1), (2, 2))
    ready(3)
    forward((3, 0), (3, 1), (3, 2), (0, 5), (1, 5), (2, 5), (3, 5))
    for i in range(X):
        hop_on(3, i)
    turn(3)
    turn(5)
    forward((0, 3), (1, 3), (2, 3), (3, 3))
    for i in range(X):
        hop_on(4, i)
    turn(4)
    forward((0, 4), (1, 4), (2, 4), (3, 4))
    for i in range(X):
        finish(i)
        backward(i, 4, i == 0)
        if i == 3:
            for piece in range(PIECES):
                pass_on(4, piece)
        backward(i, 3, i == 0)
        if i == 3:
            for piece in range(PIECES):
                pass_on(3, piece)
    for i in (3, 2, 1, 0):
        backward(i, 2, i == 3)
    backward_window(3)
    backward(3, 1, True)
    backward(3, 0, True)
    finish_dq(3)
    for piece in range(PIECES):
        pass_on(2, piece)
        i = 2 - piece * 2 // PIECES
        if piece % 2 == 0:
            backward_window(i)
            backward(i, 1, False)
        else:
            backward(i, 0, False)
            finish_dq(i)
    backward_window(0)
    backward(0, 1, False)
    backward(0, 0, False)
    for piece in range(PIECES):
        for kind in (0, 1):
            leave_sum(kind, 0, piece, partial(kind, 0, piece).astype(BF))
    finish_dq(0)
    for piece in range(PIECES):
        pass_on(1, piece)
    drain(tail_rs, 352)
    for kind, target in ((0, dkp), (1, dvp)):
        for i in range(X):
            own = tail_s[0, kind, 0] if i == 0 else tail_r[0, kind, i]
            total = own.astype(F32) + tail_r[1, kind, i].astype(F32) + tail_r[2, kind, i].astype(F32)
            fin[kind, i] = total.astype(BF)
            column = pl.multiple_of(lax.rem(x + OFF[i], X) * HD, HD)
            pltpu.make_async_copy(fin.at[kind, i], target.at[:, pl.ds(column, HD)], out_ls).start()

    drain(kv_ss, 352)
    drain(in_ss, 864)
    drain(ag_ss, 640)
    drain(rs_ss, 640)
    drain(tail_ss, 352)
    drain(out_ss, 864)
    drain(out_rs, 864)
    drain(out_ls, 416)


def hand_over(*refs):
    ins, outs, held, sems = refs[:6], refs[6:12], refs[12:18], refs[18]
    first = [pltpu.make_async_copy(ins[n], held[n], sems.at[0, n]) for n in range(6)]
    second = [pltpu.make_async_copy(held[n], outs[n], sems.at[1, n]) for n in range(6)]
    for copy in first:
        copy.start()
    for n in range(6):
        first[n].wait()
        second[n].start()
    for copy in second:
        copy.wait()


def body(q_resp, k_resp, v_resp, k_prompt, v_prompt, d_out, owner, lengths, visible):
    hbm = pl.BlockSpec(memory_space=pltpu.HBM)
    smem = pl.BlockSpec(memory_space=pltpu.SMEM)
    wide = jax.ShapeDtypeStruct((W, H * HD), BF)
    narrow = jax.ShapeDtypeStruct((W, G * HD), BF)
    shapes = (wide, wide, narrow, narrow, narrow, narrow)
    dma = pltpu.SemaphoreType.DMA
    results = pl.pallas_call(
        kernel,
        out_shape=shapes,
        in_specs=[smem] * 3 + [hbm] * 6,
        out_specs=(hbm,) * 6,
        scratch_shapes=[
            pltpu.SMEM((2, X), jnp.int32),
            pltpu.VMEM((X, W, GW), BF),
            pltpu.VMEM((X, W, GW), BF),
            pltpu.VMEM((X, W, HD), BF),
            pltpu.VMEM((X, W, HD), BF),
            pltpu.VMEM((Y, X, 2, W, HD), BF),
            pltpu.VMEM((Y, HD, CHUNK), BF),
            pltpu.VMEM((Y, HD + 16, CHUNK), BF),
            pltpu.VMEM((X, HD, ROWS), BF),
            pltpu.VMEM((X, HD, ROWS), BF),
            pltpu.VMEM((X, Y, CHUNK, ROWS), BF),
            pltpu.VMEM((X, W, ROWS), BF),
            pltpu.VMEM((X, 6, 1, ROWS), F32),
            pltpu.VMEM((X, 1, ROWS), F32),
            pltpu.VMEM((X, HD + 16, ROWS), F32),
            pltpu.VMEM((X, 8, ROWS), F32),
            pltpu.VMEM((X, HD, ROWS), F32),
            pltpu.VMEM((Y, CHUNK, HD), F32),
            pltpu.VMEM((Y, CHUNK, HD), F32),
            pltpu.VMEM((X, W, GW), BF),
            pltpu.VMEM((X, W, GW), BF),
            pltpu.VMEM((X, W, HD), BF),
            pltpu.VMEM((X, W, HD), BF),
            pltpu.VMEM((4, 2, 2, PIECES, PIECE, HD), BF),
            pltpu.VMEM((3, 2, 2, PIECES, PIECE, HD), BF),
            pltpu.VMEM((3, 2, X, W, HD), BF),
            pltpu.VMEM((3, 2, X, W, HD), BF),
            pltpu.VMEM((2, X, W, HD), BF),
            dma((4,)), dma, dma, dma((4, 3)),
            dma, dma((4, X, 2)),
            dma, dma, dma,
            dma, dma((2, PIECES, 2)),
            dma, dma,
        ],
        compiler_params=pltpu.CompilerParams(
            collective_id=0, has_side_effects=True, vmem_limit_bytes=56 * 2**20
        ),
    )(owner, lengths, visible, q_resp, k_resp, v_resp, k_prompt, v_prompt, d_out)
    return pl.pallas_call(
        hand_over,
        out_shape=shapes,
        in_specs=[hbm] * 6,
        out_specs=(hbm,) * 6,
        scratch_shapes=[pltpu.VMEM(shape.shape, BF) for shape in shapes] + [dma((2, 6))],
    )(*results)


def solution(mesh):
    rows = P(("grp", "ctx"), None)
    in_specs = (rows,) * 6 + (P("grp"),) * 3
    return jax.shard_map(
        body, mesh=mesh, in_specs=in_specs, out_specs=(rows,) * 6, check_vma=False
    )
```
